32 devices in a mesh: groups: 2 (over y), blk: 4 (over z), narrow: 4 (over x, core).
Axes of the slice: x: 2, y: 2, z: 4, core: 2. Of those that a mesh axis runs over, the one named last changes fastest.
Arguments:
- tokens: bfloat16 [256, 6144], P(('groups', 'blk'), 'narrow'), parts along dimension 0, may hold values from -6 to 6
- skip_flags: int32 [256], P(('groups', 'blk')), parts along dimension 0, may hold values from 0 to 1, as said below
- w_up: bfloat16 [6144, 24576], P('narrow', 'blk'), may hold values from -0.078125 to 0.078125
- w_down: bfloat16 [24576, 6144], P('blk', 'narrow'), may hold values from -0.0390625 to 0.0390625
Outputs:
- update: bfloat16 [256, 6144], P(('groups', 'blk'), 'narrow'), parts along dimension 0
The draws below stay inside these ranges and needn't reach their ends.
There are 2 independent parts, one for each index of `groups`. The reference program is written for one: setup_inputs(seed, part) draws one part's arguments, and reference() takes and returns one part's arrays. A program takes and returns all parts, laid end to end along the dimension named above; an argument that names none is the same for every part. Nothing has to cross between parts.
Inputs may be any that keep to these rules, and one draw needn't show every extreme that they name: `skip_flags`: in each aligned block of 32 tokens at most 24 are active (flag 0), and in every draw some block has exactly 24 active tokens.
All inputs are finite; a program needn't handle non-finite values.
Results may differ from the reference program's by a relative error of at most 0.0049.
Values may be sent and summed in bfloat16 or wider, within the bound.
A program may use at most 128 MiB of HBM per device.

```python
import jax
import jax.numpy as jnp

D = 6144
FF = 24576
TOK_BLK = 32
CAP = 24
TOKENS = 128


def draw_skip_flags(key, part):
    key = jax.random.fold_in(key, 7)
    key_count, key_fullest, key_order = jax.random.split(key, 3)
    blocks = TOKENS // TOK_BLK
    counts = jax.random.randint(key_count, (blocks,), CAP // 3, CAP + 1)
    fullest = jax.random.randint(key_fullest, (), 0, blocks)
    counts = jnp.where(jnp.arange(blocks) == fullest, CAP, counts)
    random_bits = jax.random.randint(key_order, (blocks, TOK_BLK), 0, 2 ** 20)
    scores = random_bits * TOK_BLK + jnp.arange(TOK_BLK)[None, :]
    rank_order = jnp.argsort(jnp.argsort(scores, axis=1, stable=True), axis=1, stable=True)
    active = (rank_order < counts[:, None]).astype(jnp.int32)
    return (1 - active).reshape(TOKENS).astype(jnp.int32)


def block_levels(stream_key, extent, cuts, least, top_value):
    def one(dim, blocks):
        steps = jax.random.uniform(jax.random.fold_in(jax.random.fold_in(stream_key, 6), dim), (blocks,), jnp.float32, least / len(cuts), top_value / len(cuts))
        return jnp.repeat(jnp.exp(steps), extent[dim] // blocks).reshape((-1,) + (1,) * (len(extent) - dim - 1))

    level = one(*cuts[0])
    for cut in cuts[1:]:
        level = level * one(*cut)
    return level


def scatter_about(key, extent, deviation, limit, cuts=(), kind=jnp.bfloat16):
    entries = jax.random.normal(key, extent, jnp.float32) * deviation
    if len(cuts) > 0:
        entries = block_levels(key, extent, cuts, -0.22, 0.18) * entries
    return jnp.clip(entries, min=-limit, max=limit).astype(kind)


def setup_inputs(seed: int = 0, part: int = 0) -> dict:
    splits = jax.random.split(jax.random.key(seed), 5)
    part_keys = jax.random.split(jax.random.fold_in(splits[4], part), 5)
    return {
        "tokens": scatter_about(part_keys[0], (TOKENS, D), 1.0, 6.0, ((0, 4), (1, 4))),
        "skip_flags": draw_skip_flags(jax.random.fold_in(jax.random.fold_in(splits[4], part), 71), part),
        "w_up": scatter_about(splits[2], (D, FF), D ** -0.5, 0.078125, ((0, 4), (1, 4))),
        "w_down": scatter_about(splits[3], (FF, D), FF ** -0.5, 0.0390625, ((0, 4), (1, 4))),
    }


def reference(tokens, skip_flags, w_up, w_down):
    summed = jnp.dot(tokens, w_up, preferred_element_type=jnp.float32)
    hidden = jax.nn.gelu(summed, approximate=True).astype(jnp.bfloat16)
    output = jnp.dot(hidden, w_down, preferred_element_type=jnp.float32)
    active = (1 - skip_flags).astype(jnp.float32)
    return (output * active[:, None]).astype(jnp.bfloat16)
```

```python
import functools
import math

import jax
import jax.numpy as jnp
from jax import lax
from jax.experimental import pallas as pl
from jax.experimental.pallas import tpu as pltpu
from jax.sharding import PartitionSpec as P

CAP = 24
MESH = pl.DeviceIdType.MESH
F32 = jnp.float32
BF16 = jnp.bfloat16


def gelu(v):
    return 0.5 * v * (1.0 + jnp.tanh(math.sqrt(2.0 / math.pi) * (v + 0.044715 * v * v * v)))


def remote(src, dst, send, recv, **where):
    return pltpu.make_async_remote_copy(
        src_ref=src, dst_ref=dst, send_sem=send, recv_sem=recv, device_id=where, device_id_type=MESH
    )


def kernel(
    nz, nn, nk, width,
    flags_ref, tok_ref, wup_hbm, wdn_hbm, out_ref,
    wup, wdn, xg, xs, own, sib_out, sib_in, x_out, x_in, hid, hid_in, acc, y_out, y_in,
    wup_sem, wdn_sem, tok_send, tok_recv, sib_send, sib_recv, x_send, x_recv, hid_send, hid_recv, y_send, y_recv,
):
    rows, dn = tok_ref.shape
    half = dn // 2
    nx = nn // 2
    fh = nk * width
    z = lax.axis_index("blk")
    n = lax.axis_index("narrow")
    core = lax.rem(n, 2)
    sibling = n + 1 - 2 * core
    zpeer = [lax.rem(z + d, nz) for d in range(nz)]
    xpeer = [lax.rem(n + 2 * d, nn) for d in range(nx)]

    def col(k, mine):
        base = core if mine else 1 - core
        return pl.ds(pl.multiple_of(base * fh + k * width, 128), width)

    up_copies, dn_copies = [], []
    for k in range(nk):
        for mine in (0, 1):
            s = 2 * k + mine
            up_copies.append(pltpu.make_async_copy(wup_hbm.at[:, col(k, mine)], wup.at[s], wup_sem.at[s]))
            dn_copies.append(pltpu.make_async_copy(wdn_hbm.at[col(k, mine), :], wdn.at[s], wdn_sem.at[s]))
    for c in up_copies:
        c.start()

    barrier = pltpu.get_barrier_semaphore()
    pl.semaphore_signal(barrier, inc=1, device_id={"narrow": sibling}, device_id_type=MESH)
    for p in xpeer[1:]:
        pl.semaphore_signal(barrier, inc=1, device_id={"narrow": p}, device_id_type=MESH)
    for p in zpeer[1:]:
        pl.semaphore_signal(barrier, inc=1, device_id={"blk": p}, device_id_type=MESH)

    active = (1 - flags_ref[...]).astype(F32)
    upto = (lax.broadcasted_iota(jnp.int32, (rows, rows), 0) <= lax.broadcasted_iota(jnp.int32, (rows, rows), 1))
    rank = jnp.dot(jnp.broadcast_to(active, (8, rows)).astype(BF16), upto.astype(F32).astype(BF16),
                   preferred_element_type=F32)[0:1]
    slot = (lax.broadcasted_iota(jnp.int32, (CAP, rows), 0) + 1).astype(F32)
    pick = (jnp.where(slot == jnp.broadcast_to(rank, (CAP, rows)), 1.0, 0.0)
            * jnp.broadcast_to(active, (CAP, rows))).astype(BF16)
    mine_rows = jnp.dot(pick, tok_ref[...], preferred_element_type=F32)
    xg[z] = jnp.concatenate([mine_rows[:, :half], mine_rows[:, half:]], axis=0).astype(BF16)

    pl.semaphore_wait(barrier, 1 + (nx - 1) + (nz - 1))
    for d in range(1, nz):
        remote(xg.at[z], xg.at[z], tok_send.at[d - 1], tok_recv.at[z], blk=zpeer[d]).start()
    for c in dn_copies:
        c.start()
    for d in range(1, nz):
        j = zpeer[d]
        remote(xg.at[j], xg.at[j], tok_send.at[d - 1], tok_recv.at[j], blk=zpeer[d]).wait_recv()
    left, right = [], []
    for j in range(nz):
        v = xg[j].astype(F32)
        left.append(v[:CAP])
        right.append(v[CAP:])
    xs[:, :half] = jnp.concatenate(left, axis=0).astype(BF16)
    xs[:, half:] = jnp.concatenate(right, axis=0).astype(BF16)

    def sib_copy(k):
        return remote(sib_out.at[k], sib_in.at[k], sib_send.at[k], sib_recv.at[k], narrow=sibling)

    def x_copy(k, d):
        s = k * (nx - 1) + d - 1
        return remote(x_out.at[k], x_in.at[s], x_send.at[s], x_recv.at[s], narrow=xpeer[d])

    def hid_copy(k):
        return remote(hid.at[k], hid_in.at[k], hid_send.at[k], hid_recv.at[k], narrow=sibling)

    def chip_sum(k):
        sib_copy(k).wait_recv()
        total = own[k] + sib_in[k].astype(F32)
        own[k] = total
        x_out[k] = total.astype(BF16)
        for d in range(1, nx):
            x_copy(k, d).start()

    for k in range(nk):
        up_copies[2 * k].wait()
        sib_out[k] = jnp.dot(xs[...], wup[2 * k], preferred_element_type=F32).astype(BF16)
        sib_copy(k).start()
        if k > 0:
            chip_sum(k - 1)
        up_copies[2 * k + 1].wait()
        own[k] = jnp.dot(xs[...], wup[2 * k + 1], preferred_element_type=F32)
    chip_sum(nk - 1)

    for k in range(nk):
        total = own[k]
        for d in range(1, nx):
            x_copy(k, d).wait_recv()
            total = total + x_in[k * (nx - 1) + d - 1].astype(F32)
        hid[k] = gelu(total).astype(BF16)
        hid_copy(k).start()
        dn_copies[2 * k + 1].wait()
        term = jnp.dot(hid[k], wdn[2 * k + 1], preferred_element_type=F32)
        if k == 0:
            acc[...] = term
        else:
            acc[...] += term
        dn_copies[2 * k].wait()
        hid_copy(k).wait_recv()
        acc[...] += jnp.dot(hid_in[k], wdn[2 * k], preferred_element_type=F32)

    for j in range(nz):
        v = acc[CAP * j:CAP * (j + 1), :]
        y_out[j] = jnp.concatenate([v[:, :half], v[:, half:]], axis=0).astype(BF16)

    def y_copy(d):
        return remote(y_out.at[zpeer[d]], y_in.at[d - 1], y_send.at[d - 1], y_recv.at[d - 1], blk=zpeer[d])

    for d in range(1, nz):
        y_copy(d).start()
    mine = acc[pl.ds(pl.multiple_of(z * CAP, 8), CAP), :]
    total = jnp.concatenate([mine[:, :half], mine[:, half:]], axis=0)
    for d in range(1, nz):
        y_copy(d).wait_recv()
        total = total + y_in[d - 1].astype(F32)
    total = jnp.concatenate([total[:CAP], total[CAP:]], axis=1).astype(BF16)
    out_ref[...] = lax.dot_general(
        pick, total, (((0,), (0,)), ((), ())), preferred_element_type=F32
    ).astype(BF16)

    for d in range(1, nz):
        remote(xg.at[z], xg.at[z], tok_send.at[d - 1], tok_recv.at[z], blk=zpeer[d]).wait_send()
        y_copy(d).wait_send()
    for k in range(nk):
        sib_copy(k).wait_send()
        hid_copy(k).wait_send()
        for d in range(1, nx):
            x_copy(k, d).wait_send()


def shards(nz, nn, tokens, skip_flags, w_up, w_down):
    rows, dn = tokens.shape
    ff = w_up.shape[1]
    fh = ff // 2
    width = 512 if fh % 512 == 0 else 128
    nk = fh // width
    nx = nn // 2
    total = CAP * nz
    vmem, dma = pltpu.VMEM, pltpu.SemaphoreType.DMA
    return pl.pallas_call(
        functools.partial(kernel, nz, nn, nk, width),
        out_shape=jax.ShapeDtypeStruct((rows, dn), BF16),
        in_specs=[pl.BlockSpec(memory_space=pltpu.VMEM)] * 2 + [pl.BlockSpec(memory_space=pl.ANY)] * 2,
        out_specs=pl.BlockSpec(memory_space=pltpu.VMEM),
        scratch_shapes=[
            vmem((2 * nk, dn, width), BF16),
            vmem((2 * nk, width, dn), BF16),
            vmem((nz, 2 * CAP, dn // 2), BF16),
            vmem((total, dn), BF16),
            vmem((nk, total, width), F32),
            vmem((nk, total, width), BF16),
            vmem((nk, total, width), BF16),
            vmem((nk, total, width), BF16),
            vmem((nk * (nx - 1), total, width), BF16),
            vmem((nk, total, width), BF16),
            vmem((nk, total, width), BF16),
            vmem((total, dn), F32),
            vmem((nz, 2 * CAP, dn // 2), BF16),
            vmem((nz - 1, 2 * CAP, dn // 2), BF16),
            dma((2 * nk,)), dma((2 * nk,)),
            dma((nz - 1,)), dma((nz,)),
            dma((nk,)), dma((nk,)),
            dma((nk * (nx - 1),)), dma((nk * (nx - 1),)),
            dma((nk,)), dma((nk,)),
            dma((nz - 1,)), dma((nz - 1,)),
        ],
        compiler_params=pltpu.CompilerParams(
            collective_id=0, has_side_effects=True, vmem_limit_bytes=60 * 2 ** 20
        ),
        cost_estimate=pl.CostEstimate(
            flops=4 * total * dn * ff, bytes_accessed=4 * dn * ff, transcendentals=total * fh
        ),
    )(skip_flags.reshape(1, rows), tokens, w_up, w_down)


def solution(mesh):
    in_specs = (
        P(("groups", "blk"), "narrow"),
        P(("groups", "blk")),
        P("narrow", "blk"),
        P("blk", "narrow"),
    )
    out_specs = P(("groups", "blk"), "narrow")
    body = functools.partial(shards, mesh.shape["blk"], mesh.shape["narrow"])
    return jax.shard_map(body, mesh=mesh, in_specs=in_specs, out_specs=out_specs, check_vma=False)
```

```python
import functools
import math

import jax
import jax.numpy as jnp
from jax import lax
from jax.experimental import pallas as pl
from jax.experimental.pallas import tpu as pltpu
from jax.sharding import PartitionSpec as P

CAP = 24
MESH = pl.DeviceIdType.MESH
F32 = jnp.float32
BF16 = jnp.bfloat16


def gelu(v):
    return 0.5 * v * (1.0 + jnp.tanh(math.sqrt(2.0 / math.pi) * (v + 0.044715 * v * v * v)))


def remote(src, dst, send, recv, **where):
    return pltpu.make_async_remote_copy(
        src_ref=src, dst_ref=dst, send_sem=send, recv_sem=recv, device_id=where, device_id_type=MESH
    )


def fold(v):
    middle = v.shape[1] // 2
    return jnp.concatenate([v[:, :middle], v[:, middle:]], axis=0)


def unfold(v):
    middle = v.shape[0] // 2
    return jnp.concatenate([v[:middle], v[middle:]], axis=1)


def kernel(
    nz, nn, nk, width, groups,
    flags_ref, tok_ref, wup_hbm, wdn_hbm, out_ref,
    wup, wdn, xg, xs, own, sib_out, sib_in, x_out, x_in, hid, hid_in, acc, y_out, y_in,
    wup_sem, wdn_sem, tok_send, tok_recv, sib_send, sib_recv, x_send, x_recv, hid_send, hid_recv, y_send, y_recv,
):
    rows, dn = tok_ref.shape
    half = dn // 2
    nx = nn // 2
    fh = nk * width
    z = lax.axis_index("blk")
    n = lax.axis_index("narrow")
    core = lax.rem(n, 2)
    sibling = n + 1 - 2 * core
    xpeer = [lax.rem(n + 2 * d, nn) for d in range(nx)]

    order = [z]
    for i in range(1, nz // 2):
        j = lax.rem(z + 2 * i, nz)
        order += [j, j + 1 - 2 * lax.rem(j, 2)]
    order.append(z + 1 - 2 * lax.rem(z, 2))
    ng = len(groups)
    members = CAP * len(groups[0])
    steps = ng * nk

    def col(k, mine):
        base = core if mine else 1 - core
        return pl.ds(pl.multiple_of(base * fh + k * width, 128), width)

    up_copies, dn_copies = [], []
    for k in range(nk):
        for mine in (0, 1):
            s = 2 * k + mine
            up_copies.append(pltpu.make_async_copy(wup_hbm.at[:, col(k, mine)], wup.at[s], wup_sem.at[s]))
            dn_copies.append(pltpu.make_async_copy(wdn_hbm.at[col(k, mine), :], wdn.at[s], wdn_sem.at[s]))
    for c in up_copies:
        c.start()

    barrier = pltpu.get_barrier_semaphore()
    pl.semaphore_signal(barrier, inc=1, device_id={"narrow": sibling}, device_id_type=MESH)
    for p in xpeer[1:]:
        pl.semaphore_signal(barrier, inc=1, device_id={"narrow": p}, device_id_type=MESH)
    for p in order[1:]:
        pl.semaphore_signal(barrier, inc=1, device_id={"blk": p}, device_id_type=MESH)

    active = (1 - flags_ref[...]).astype(F32)
    upto = (lax.broadcasted_iota(jnp.int32, (rows, rows), 0) <= lax.broadcasted_iota(jnp.int32, (rows, rows), 1))
    rank = jnp.dot(jnp.broadcast_to(active, (8, rows)).astype(BF16), upto.astype(F32).astype(BF16),
                   preferred_element_type=F32)[0:1]
    slot = (lax.broadcasted_iota(jnp.int32, (CAP, rows), 0) + 1).astype(F32)
    pick = (jnp.where(slot == jnp.broadcast_to(rank, (CAP, rows)), 1.0, 0.0)
            * jnp.broadcast_to(active, (CAP, rows))).astype(BF16)
    mine_rows = jnp.dot(pick, tok_ref[...], preferred_element_type=F32)
    xg[z] = fold(mine_rows).astype(BF16)

    def tok_copy(p):
        return remote(xg.at[z], xg.at[z], tok_send.at[p], tok_recv.at[z], blk=order[p])

    pl.semaphore_wait(barrier, 1 + (nx - 1) + (nz - 1))
    for p in range(nz - 1, 0, -1):
        tok_copy(p).start()
    for c in dn_copies:
        c.start()

    def sib_copy(s):
        return remote(sib_out.at[s], sib_in.at[s], sib_send.at[s], sib_recv.at[s], narrow=sibling)

    def x_copy(s, d):
        q = s * (nx - 1) + d - 1
        return remote(x_out.at[q], x_in.at[q], x_send.at[q], x_recv.at[q], narrow=xpeer[d])

    def hid_copy(s):
        part = (s % nk, pl.ds(s // nk * members, members))
        return remote(hid.at[part], hid_in.at[part], hid_send.at[s], hid_recv.at[s], narrow=sibling)

    def y_copy(p):
        return remote(y_out.at[p], y_in.at[z], y_send.at[p], y_recv.at[z], blk=order[p])

    def gather(g):
        found = []
        for p in groups[g]:
            j = order[p]
            if p > 0:
                remote(xg.at[j], xg.at[j], tok_send.at[p], tok_recv.at[j], blk=j).wait_recv()
            found.append(unfold(xg[j].astype(F32)))
        xs[g] = jnp.concatenate(found, axis=0).astype(BF16)

    def up(s):
        g, k = divmod(s, nk)
        if k == 0:
            gather(g)
        if g == 0:
            up_copies[2 * k].wait()
        sib_out[s] = jnp.dot(xs[g], wup[2 * k], preferred_element_type=F32).astype(BF16)
        sib_copy(s).start()
        if g == 0:
            up_copies[2 * k + 1].wait()
        own[s] = jnp.dot(xs[g], wup[2 * k + 1], preferred_element_type=F32)

    def chip_sum(s):
        sib_copy(s).wait_recv()
        total = own[s] + sib_in[s].astype(F32)
        own[s] = total
        for d in range(1, nx):
            x_out[s * (nx - 1) + d - 1] = total.astype(BF16)
            x_copy(s, d).start()

    def act(s):
        g, k = divmod(s, nk)
        total = own[s]
        for d in range(1, nx):
            x_copy(s, d).wait_recv()
            total = total + x_in[s * (nx - 1) + d - 1].astype(F32)
        hid[k, g * members:(g + 1) * members] = gelu(total).astype(BF16)
        hid_copy(s).start()

    def down(k):
        dn_copies[2 * k + 1].wait()
        term = jnp.dot(hid[k], wdn[2 * k + 1], preferred_element_type=F32)
        if k == 0:
            acc[...] = term
        else:
            acc[...] += term
        dn_copies[2 * k].wait()
        for g in range(ng):
            hid_copy(g * nk + k).wait_recv()
        acc[...] += jnp.dot(hid_in[k], wdn[2 * k], preferred_element_type=F32)

    lag = nk
    for t in range(steps + lag):
        if t < steps:
            up(t)
        if 1 <= t <= steps:
            chip_sum(t - 1)
        s = t - lag
        if s >= 0:
            act(s)
            if s // nk == ng - 1:
                down(s % nk)

    places = [p for group in groups for p in group]
    for p in range(1, nz):
        i = CAP * places.index(p)
        y_out[p] = fold(acc[i:i + CAP, :]).astype(BF16)
        y_copy(p).start()
    base = CAP * places.index(0)
    total = fold(acc[base:base + CAP, :])
    for p in range(1, nz):
        j = order[p]
        remote(y_out.at[p], y_in.at[j], y_send.at[p], y_recv.at[j], blk=j).wait_recv()
        total = total + y_in[j].astype(F32)
    out_ref[...] = lax.dot_general(
        pick, unfold(total).astype(BF16), (((0,), (0,)), ((), ())), preferred_element_type=F32
    ).astype(BF16)

    for p in range(1, nz):
        tok_copy(p).wait_send()
        y_copy(p).wait_send()
    for s in range(steps):
        sib_copy(s).wait_send()
        hid_copy(s).wait_send()
        for d in range(1, nx):
            x_copy(s, d).wait_send()


def shards(nz, nn, tokens, skip_flags, w_up, w_down):
    rows, dn = tokens.shape
    ff = w_up.shape[1]
    fh = ff // 2
    groups = [[0, nz - 1], list(range(1, nz - 1))] if nz == 4 else [list(range(nz))]
    width = 512 if fh % 512 == 0 else 128
    nk = fh // width
    nx = nn // 2
    total = CAP * nz
    ng = len(groups)
    steps = ng * nk
    members = total // ng
    shape = (members, width)
    vmem, dma = pltpu.VMEM, pltpu.SemaphoreType.DMA
    return pl.pallas_call(
        functools.partial(kernel, nz, nn, nk, width, groups),
        out_shape=jax.ShapeDtypeStruct((rows, dn), BF16),
        in_specs=[pl.BlockSpec(memory_space=pltpu.VMEM)] * 2 + [pl.BlockSpec(memory_space=pl.ANY)] * 2,
        out_specs=pl.BlockSpec(memory_space=pltpu.VMEM),
        scratch_shapes=[
            vmem((2 * nk, dn, width), BF16),
            vmem((2 * nk, width, dn), BF16),
            vmem((nz, 2 * CAP, dn // 2), BF16),
            vmem((ng, members, dn), BF16),
            vmem((steps,) + shape, F32),
            vmem((steps,) + shape, BF16),
            vmem((steps,) + shape, BF16),
            vmem((steps * (nx - 1),) + shape, BF16),
            vmem((steps * (nx - 1),) + shape, BF16),
            vmem((nk, total, width), BF16),
            vmem((nk, total, width), BF16),
            vmem((total, dn), F32),
            vmem((nz, 2 * CAP, dn // 2), BF16),
            vmem((nz, 2 * CAP, dn // 2), BF16),
            dma((2 * nk,)), dma((2 * nk,)),
            dma((nz,)), dma((nz,)),
            dma((steps,)), dma((steps,)),
            dma((steps * (nx - 1),)), dma((steps * (nx - 1),)),
            dma((steps,)), dma((steps,)),
            dma((nz,)), dma((nz,)),
        ],
        compiler_params=pltpu.CompilerParams(
            collective_id=0, has_side_effects=True, vmem_limit_bytes=60 * 2 ** 20
        ),
        cost_estimate=pl.CostEstimate(
            flops=4 * total * dn * ff, bytes_accessed=4 * dn * ff, transcendentals=total * fh
        ),
    )(skip_flags.reshape(1, rows), tokens, w_up, w_down)


def solution(mesh):
    in_specs = (
        P(("groups", "blk"), "narrow"),
        P(("groups", "blk")),
        P("narrow", "blk"),
        P("blk", "narrow"),
    )
    out_specs = P(("groups", "blk"), "narrow")
    body = functools.partial(shards, mesh.shape["blk"], mesh.shape["narrow"])
    return jax.shard_map(body, mesh=mesh, in_specs=in_specs, out_specs=out_specs, check_vma=False)
```

```python
import functools
import math

import jax
import jax.numpy as jnp
from jax import lax
from jax.experimental import pallas as pl
from jax.experimental.pallas import tpu as pltpu
from jax.sharding import PartitionSpec as P

CAP = 24
MESH = pl.DeviceIdType.MESH
F32 = jnp.float32
BF16 = jnp.bfloat16


def gelu(v):
    return 0.5 * v * (1.0 + jnp.tanh(math.sqrt(2.0 / math.pi) * (v + 0.044715 * v * v * v)))


def remote(src, dst, send, recv, **where):
    return pltpu.make_async_remote_copy(
        src_ref=src, dst_ref=dst, send_sem=send, recv_sem=recv, device_id=where, device_id_type=MESH
    )


def fold(v):
    middle = v.shape[1] // 2
    return jnp.concatenate([v[:, :middle], v[:, middle:]], axis=0)


def unfold(v):
    middle = v.shape[0] // 2
    return jnp.concatenate([v[:middle], v[middle:]], axis=1)


def kernel(
    nz, nn, nk, width, groups,
    flags_ref, tok_ref, wup_hbm, wdn_hbm, out_ref,
    wup, wdn, xg, xs, own, sib_out, sib_in, x_out, x_in, hid, hid_in, acc, y_out, y_in,
    wup_sem, wdn_sem, tok_send, tok_recv, sib_send, sib_recv, x_send, x_recv, hid_send, hid_recv, y_send, y_recv,
):
    rows, dn = tok_ref.shape
    half = dn // 2
    nx = nn // 2
    fh = nk * width
    z = lax.axis_index("blk")
    n = lax.axis_index("narrow")
    core = lax.rem(n, 2)
    sibling = n + 1 - 2 * core
    xpeer = [lax.rem(n + 2 * d, nn) for d in range(nx)]

    order = [z]
    for i in range(1, nz // 2):
        j = lax.rem(z + 2 * i, nz)
        order += [j, j + 1 - 2 * lax.rem(j, 2)]
    order.append(z + 1 - 2 * lax.rem(z, 2))
    ng = len(groups)
    members = CAP * len(groups[0])
    steps = ng * nk

    def col(k, mine):
        base = core if mine else 1 - core
        return pl.ds(pl.multiple_of(base * fh + k * width, 128), width)

    up_copies, dn_copies = [], []
    for k in range(nk):
        for mine in (0, 1):
            s = 2 * k + mine
            up_copies.append(pltpu.make_async_copy(wup_hbm.at[:, col(k, mine)], wup.at[s], wup_sem.at[s]))
            dn_copies.append(pltpu.make_async_copy(wdn_hbm.at[col(k, mine), :], wdn.at[s], wdn_sem.at[s]))
    for c in up_copies:
        c.start()

    barrier = pltpu.get_barrier_semaphore()
    pl.semaphore_signal(barrier, inc=1, device_id={"narrow": sibling}, device_id_type=MESH)
    for p in xpeer[1:]:
        pl.semaphore_signal(barrier, inc=1, device_id={"narrow": p}, device_id_type=MESH)
    for p in order[1:]:
        pl.semaphore_signal(barrier, inc=1, device_id={"blk": p}, device_id_type=MESH)

    active = (1 - flags_ref[...]).astype(F32)
    upto = (lax.broadcasted_iota(jnp.int32, (rows, rows), 0) <= lax.broadcasted_iota(jnp.int32, (rows, rows), 1))
    rank = jnp.dot(jnp.broadcast_to(active, (8, rows)).astype(BF16), upto.astype(F32).astype(BF16),
                   preferred_element_type=F32)[0:1]
    slot = (lax.broadcasted_iota(jnp.int32, (CAP, rows), 0) + 1).astype(F32)
    pick = (jnp.where(slot == jnp.broadcast_to(rank, (CAP, rows)), 1.0, 0.0)
            * jnp.broadcast_to(active, (CAP, rows))).astype(BF16)
    mine_rows = jnp.dot(pick, tok_ref[...], preferred_element_type=F32)
    xg[z] = fold(mine_rows).astype(BF16)

    def tok_copy(p):
        return remote(xg.at[z], xg.at[z], tok_send.at[p], tok_recv.at[z], blk=order[p])

    pl.semaphore_wait(barrier, 1 + (nx - 1) + (nz - 1))
    for p in range(nz - 1, 0, -1):
        tok_copy(p).start()
    for c in dn_copies:
        c.start()

    def sib_copy(s):
        return remote(sib_out.at[s], sib_in.at[s], sib_send.at[s], sib_recv.at[s], narrow=sibling)

    def x_copy(s, d):
        q = s * (nx - 1) + d - 1
        return remote(x_out.at[q], x_in.at[q], x_send.at[q], x_recv.at[q], narrow=xpeer[d])

    def hid_copy(s):
        part = (s % nk, pl.ds(s // nk * members, members))
        return remote(hid.at[part], hid_in.at[part], hid_send.at[s], hid_recv.at[s], narrow=sibling)

    def y_copy(p):
        return remote(y_out.at[p], y_in.at[z], y_send.at[p], y_recv.at[z], blk=order[p])

    def gather(g):
        found = []
        for p in groups[g]:
            j = order[p]
            if p > 0:
                remote(xg.at[j], xg.at[j], tok_send.at[p], tok_recv.at[j], blk=j).wait_recv()
            found.append(unfold(xg[j].astype(F32)))
        xs[g] = jnp.concatenate(found, axis=0).astype(BF16)

    def up(s):
        g, k = divmod(s, nk)
        if k == 0:
            gather(g)
        if g == 0:
            up_copies[2 * k].wait()
        sib_out[s] = jnp.dot(xs[g], wup[2 * k], preferred_element_type=F32).astype(BF16)
        sib_copy(s).start()
        if s > 0:
            chip_sum(s - 1)
        if g == 0:
            up_copies[2 * k + 1].wait()
        own[s] = jnp.dot(xs[g], wup[2 * k + 1], preferred_element_type=F32)

    def chip_sum(s):
        sib_copy(s).wait_recv()
        total = own[s] + sib_in[s].astype(F32)
        own[s] = total
        for d in range(1, nx):
            x_out[s * (nx - 1) + d - 1] = total.astype(BF16)
            x_copy(s, d).start()

    def act(s):
        g, k = divmod(s, nk)
        total = own[s]
        for d in range(1, nx):
            x_copy(s, d).wait_recv()
            total = total + x_in[s * (nx - 1) + d - 1].astype(F32)
        hid[k, g * members:(g + 1) * members] = gelu(total).astype(BF16)
        hid_copy(s).start()

    def down(k):
        dn_copies[2 * k + 1].wait()
        term = jnp.dot(hid[k], wdn[2 * k + 1], preferred_element_type=F32)
        if k == 0:
            acc[...] = term
        else:
            acc[...] += term
        dn_copies[2 * k].wait()
        for g in range(ng):
            hid_copy(g * nk + k).wait_recv()
        acc[...] += jnp.dot(hid_in[k], wdn[2 * k], preferred_element_type=F32)

    lag = nk
    for t in range(steps + lag):
        if t < steps:
            up(t)
        if t == steps:
            chip_sum(t - 1)
        s = t - lag
        if s >= 0:
            act(s)
            if s // nk == ng - 1:
                down(s % nk)

    places = [p for group in groups for p in group]
    for p in range(1, nz):
        i = CAP * places.index(p)
        y_out[p] = fold(acc[i:i + CAP, :]).astype(BF16)
        y_copy(p).start()
    base = CAP * places.index(0)
    total = fold(acc[base:base + CAP, :])
    for p in range(1, nz):
        j = order[p]
        remote(y_out.at[p], y_in.at[j], y_send.at[p], y_recv.at[j], blk=j).wait_recv()
        total = total + y_in[j].astype(F32)
    out_ref[...] = lax.dot_general(
        pick, unfold(total).astype(BF16), (((0,), (0,)), ((), ())), preferred_element_type=F32
    ).astype(BF16)

    for p in range(1, nz):
        tok_copy(p).wait_send()
        y_copy(p).wait_send()
    for s in range(steps):
        sib_copy(s).wait_send()
        hid_copy(s).wait_send()
        for d in range(1, nx):
            x_copy(s, d).wait_send()


def shards(nz, nn, tokens, skip_flags, w_up, w_down):
    rows, dn = tokens.shape
    ff = w_up.shape[1]
    fh = ff // 2
    groups = [[0, nz - 1], list(range(1, nz - 1))] if nz == 4 else [list(range(nz))]
    width = 512 if fh % 512 == 0 else 128
    nk = fh // width
    nx = nn // 2
    total = CAP * nz
    ng = len(groups)
    steps = ng * nk
    members = total // ng
    shape = (members, width)
    vmem, dma = pltpu.VMEM, pltpu.SemaphoreType.DMA
    return pl.pallas_call(
        functools.partial(kernel, nz, nn, nk, width, groups),
        out_shape=jax.ShapeDtypeStruct((rows, dn), BF16),
        in_specs=[pl.BlockSpec(memory_space=pltpu.VMEM)] * 2 + [pl.BlockSpec(memory_space=pl.ANY)] * 2,
        out_specs=pl.BlockSpec(memory_space=pltpu.VMEM),
        scratch_shapes=[
            vmem((2 * nk, dn, width), BF16),
            vmem((2 * nk, width, dn), BF16),
            vmem((nz, 2 * CAP, dn // 2), BF16),
            vmem((ng, members, dn), BF16),
            vmem((steps,) + shape, F32),
            vmem((steps,) + shape, BF16),
            vmem((steps,) + shape, BF16),
            vmem((steps * (nx - 1),) + shape, BF16),
            vmem((steps * (nx - 1),) + shape, BF16),
            vmem((nk, total, width), BF16),
            vmem((nk, total, width), BF16),
            vmem((total, dn), F32),
            vmem((nz, 2 * CAP, dn // 2), BF16),
            vmem((nz, 2 * CAP, dn // 2), BF16),
            dma((2 * nk,)), dma((2 * nk,)),
            dma((nz,)), dma((nz,)),
            dma((steps,)), dma((steps,)),
            dma((steps * (nx - 1),)), dma((steps * (nx - 1),)),
            dma((steps,)), dma((steps,)),
            dma((nz,)), dma((nz,)),
        ],
        compiler_params=pltpu.CompilerParams(
            collective_id=0, has_side_effects=True, vmem_limit_bytes=60 * 2 ** 20
        ),
        cost_estimate=pl.CostEstimate(
            flops=4 * total * dn * ff, bytes_accessed=4 * dn * ff, transcendentals=total * fh
        ),
    )(skip_flags.reshape(1, rows), tokens, w_up, w_down)


def solution(mesh):
    in_specs = (
        P(("groups", "blk"), "narrow"),
        P(("groups", "blk")),
        P("narrow", "blk"),
        P("blk", "narrow"),
    )
    out_specs = P(("groups", "blk"), "narrow")
    body = functools.partial(shards, mesh.shape["blk"], mesh.shape["narrow"])
    return jax.shard_map(body, mesh=mesh, in_specs=in_specs, out_specs=out_specs, check_vma=False)
```
